32 devices in a mesh: section: 2 (over x), dp: 16 (over z, y, core).
Axes of the slice: x: 2, y: 2, z: 4, core: 2. Of those that a mesh axis runs over, the one named last changes fastest.
Arguments:
- hidden: bfloat16 [32, 256, 3584], P(('section', 'dp')), may hold values from -1000 to 1000, as said below
- lengths: int32 [32], P(('section', 'dp')), may hold values from 64 to 256, as said below
- pair_perm: int32 [16], replicated, may hold values from 0 to 15, as said below
- norm_gain: bfloat16 [3584], replicated, may hold values from 0.099609375 to 1.8984375
- projection: bfloat16 [3584, 1024], replicated, may hold values from -0.09375 to 0.09375
Outputs:
- hidden_grad: bfloat16 [32, 256, 3584], P(('section', 'dp'))
- loss: float32 [], replicated
The draws below stay inside these ranges and needn't reach their ends.
Inputs may be any that keep to these rules, and one draw needn't show every extreme that they name: hidden rows of the encoder, finite. `lengths`: every sequence holds at least 64 valid tokens, and some sequence fills all 256 positions. `pair_perm`: a permutation: each docstring is paired with exactly one code.
All inputs are finite; a program needn't handle non-finite values.
Results may differ from the reference program's by a relative error of at most 0.008.
Values may be sent and summed in bfloat16 or wider, within the bound.
No kernel may reach another device: no remote copies, remote signals or barrier semaphores. Data moves between devices by JAX's collectives and lax.ppermute only.
A program may use at most 64 MiB of HBM per device.

```python
import jax
import jax.numpy as jnp
from jax import lax

D = 3584
E = 1024
LEN = 256
SEQS = 32
PAIRS = 16


def shared_perm(key):
    return jax.random.permutation(jax.random.fold_in(key, 11), PAIRS).astype(jnp.int32)


def draw_pair_perm(key, part):
    return shared_perm(key)


def draw_hidden(key, part):
    perm = shared_perm(key)
    inverse = jnp.zeros((PAIRS,), jnp.int32).at[perm].set(jnp.arange(PAIRS, dtype=jnp.int32))
    pair_of = jnp.concatenate([jnp.arange(PAIRS, dtype=jnp.int32), inverse]).astype(jnp.int32)
    cluster_of = (pair_of // 4).astype(jnp.int32)
    keys = jax.random.split(jax.random.fold_in(key, 5), 10)
    pair_dirs = jax.random.normal(keys[0], (PAIRS, D), jnp.float32)
    cluster_dirs = jax.random.normal(keys[1], (PAIRS, D), jnp.float32)
    batch_dir = jax.random.normal(keys[2], (1, D), jnp.float32)
    own_dirs = jax.random.normal(keys[3], (SEQS, D), jnp.float32)
    seq_pos = jnp.arange(SEQS, dtype=jnp.float32) / SEQS
    pair_weight = jax.random.uniform(keys[4], (PAIRS,), jnp.float32, 0.18, 0.3)
    cluster_weight = jax.random.uniform(keys[5], (PAIRS,), jnp.float32, 0.15, 0.3)
    common_weight = jax.random.uniform(keys[6], (SEQS,), jnp.float32, 0.0, 1.0) * (0.2 + 0.4 * seq_pos)
    base = jax.random.normal(keys[7], (SEQS, LEN, D), jnp.float32)
    component = pair_weight[pair_of][:, None] * pair_dirs[pair_of]
    component = component + cluster_weight[cluster_of][:, None] * cluster_dirs[cluster_of]
    component = component + common_weight[:, None] * batch_dir + 0.5 * own_dirs
    row_scales = jnp.exp(jax.random.uniform(keys[8], (SEQS, LEN, 1), jnp.float32, 0.0, 2.3))
    chan_scales = jnp.exp(jax.random.uniform(keys[9], (1, 1, D), jnp.float32, 0.0, 2.3))
    mixed = jnp.clip(base + component[:, None, :], -8.0, 8.0)
    return (mixed * row_scales * chan_scales).astype(jnp.bfloat16)


def draw_lengths(key, part):
    key_len, key_spot = jax.random.split(jax.random.fold_in(key, 7))
    shortest = max(1, LEN // 4)
    drawn_lengths = jax.random.randint(key_len, (SEQS,), shortest, LEN + 1, dtype=jnp.int32)
    longest_at = jax.random.randint(key_spot, (), 0, SEQS, dtype=jnp.int32)
    return jnp.where(jnp.arange(SEQS, dtype=jnp.int32) == longest_at, LEN, drawn_lengths).astype(jnp.int32)


def gaussian(own_key, shape, spread, bound, kind=jnp.bfloat16):
    return jnp.clip(spread * jax.random.normal(own_key, shape, jnp.float32), -bound, bound).astype(kind)


def setup_inputs(seed: int = 0) -> dict:
    key_list = jax.random.split(jax.random.key(seed), 6)
    return {
        "hidden": draw_hidden(jax.random.fold_in(key_list[5], 71), 0),
        "lengths": draw_lengths(jax.random.fold_in(key_list[5], 71), 0),
        "pair_perm": draw_pair_perm(jax.random.fold_in(key_list[5], 71), 0),
        "norm_gain": jnp.clip(1.0 + 0.18 * jax.random.normal(key_list[3], (D,), jnp.float32), 0.099609375, 1.8984375).astype(jnp.bfloat16),
        "projection": gaussian(key_list[4], (D, E), D ** -0.5, 0.09375),
    }


inv_temp = 20.0
loss_scale = 1024.0
norm_eps = 1e-06

def partners(pair_perm):
    pair_count = pair_perm.shape[0]
    order_ids = jnp.arange(pair_count, dtype=jnp.int32)
    inverse = jnp.zeros((pair_count,), jnp.int32).at[pair_perm].set(order_ids)
    return jnp.concatenate([pair_perm + pair_count, inverse]).astype(jnp.int32)

def pool_one(seq_rows, length, gain_f):
    values = seq_rows.astype(jnp.float32)
    inv_rms = lax.rsqrt(lax.optimization_barrier(jnp.mean(values * values, axis=1)) + norm_eps)
    share = (jnp.arange(seq_rows.shape[0], dtype=jnp.int32) < length).astype(jnp.float32) / length.astype(jnp.float32)
    return lax.optimization_barrier(jnp.sum((share * inv_rms)[:, None] * values, axis=0)) * gain_f

def back_one(seq_rows, length, scaled):
    values = seq_rows.astype(jnp.float32)
    inv_rms = lax.rsqrt(lax.optimization_barrier(jnp.mean(values * values, axis=1)) + norm_eps)
    share = (jnp.arange(seq_rows.shape[0], dtype=jnp.int32) < length).astype(jnp.float32) / length.astype(jnp.float32)
    dot_rows = lax.optimization_barrier(jnp.sum(values * scaled[None, :], axis=1))
    result = share[:, None] * (inv_rms[:, None] * scaled[None, :] - values * (inv_rms ** 3 * dot_rows / seq_rows.shape[1])[:, None])
    return result.astype(jnp.bfloat16)

def reference(hidden, lengths, pair_perm, norm_gain, projection):
    gain_f = norm_gain.astype(jnp.float32)
    seq_count = hidden.shape[0]
    pair_count = seq_count // 2
    pooled = lax.map(lambda item: pool_one(item[0], item[1], gain_f), (hidden, lengths)).astype(jnp.bfloat16)
    raw_emb = jnp.dot(pooled, projection, preferred_element_type=jnp.float32)
    magnitude = jnp.sqrt(lax.optimization_barrier(jnp.sum(raw_emb * raw_emb, axis=1, keepdims=True)) + norm_eps)
    unit = raw_emb / magnitude
    emb = unit.astype(jnp.bfloat16)
    codes = emb[:pair_count]
    docs = emb[pair_count:]
    scores = inv_temp * jnp.dot(codes, docs.T, preferred_element_type=jnp.float32)
    exp_scores = jnp.exp(scores)
    code_totals = lax.optimization_barrier(jnp.sum(exp_scores, axis=1))
    doc_totals = lax.optimization_barrier(jnp.sum(exp_scores, axis=0))
    columns = jnp.arange(pair_count, dtype=jnp.int32)
    target = (columns[None, :] == pair_perm[:, None]).astype(jnp.float32)
    loss = (jnp.sum(jnp.log(code_totals)) + jnp.sum(jnp.log(doc_totals)) - 2.0 * jnp.sum(target * scores)) / seq_count
    factors = exp_scores / code_totals[:, None] + exp_scores / doc_totals[None, :] - 2.0 * target
    factor = loss_scale * inv_temp
    grad_codes = factor * jnp.dot(factors, docs.astype(jnp.float32), precision=lax.Precision.HIGHEST)
    grad_docs = factor * jnp.dot(factors.T, codes.astype(jnp.float32), precision=lax.Precision.HIGHEST)
    demb = jnp.concatenate([grad_codes, grad_docs], axis=0)
    projected = lax.optimization_barrier(jnp.sum(unit * demb, axis=1, keepdims=True))
    grad_raw = ((demb - unit * projected) / magnitude).astype(jnp.bfloat16)
    grad_pooled = jnp.dot(grad_raw, projection.T, preferred_element_type=jnp.float32)
    scaled = grad_pooled * gain_f[None, :]
    hidden_grad = lax.map(lambda item: back_one(item[0], item[1], item[2]), (hidden, lengths, scaled))
    return (hidden_grad, loss)
```

```python
import functools

import jax
import jax.numpy as jnp
from jax import lax
from jax.experimental import pallas as pl
from jax.experimental.pallas import tpu as pltpu
from jax.sharding import PartitionSpec as P

inv_temp = 20.0
loss_scale = 1024.0
norm_eps = 1e-06
both = ("section", "dp")

lane = 128
hidden_parts = 4
proj_rows = 512
out_rows = 64
group = 32
back_rows = 768
mxu_rows = 256


def parts_of(total, count):
    step = total // count
    return [pl.ds(i * step, step) for i in range(count)]


def tall_parts(total, tall_rows):
    cuts = [(at, min(tall_rows, total - at)) for at in range(0, total, tall_rows)]
    at, tall = cuts.pop()
    return cuts + [(at, tall // 2), (at + tall // 2, tall - tall // 2)]


def three_parts(x):
    high = x.astype(jnp.bfloat16).astype(jnp.float32)
    middle = (x - high).astype(jnp.bfloat16).astype(jnp.float32)
    low = (x - high - middle).astype(jnp.bfloat16).astype(jnp.float32)
    return high, middle, low


def pool_kernel(
    length_ref, gain_ref, hidden_ref, proj_ref,
    copies_ref, raw_ref, squares_ref, scale_ref, rows, weights,
    gain_at, rows_sem, weights_sem, gain_sem,
):
    seq_len, width = rows.shape
    emb_width = weights.shape[1]
    gain_copy = pltpu.make_async_copy(gain_ref, gain_at, gain_sem)
    row_cuts = parts_of(seq_len, hidden_parts)
    proj_cuts = tall_parts(width, proj_rows)
    row_copies = [
        pltpu.make_async_copy(hidden_ref.at[0, cut], rows.at[cut], rows_sem.at[i])
        for i, cut in enumerate(row_cuts)
    ]
    proj_copies = [
        pltpu.make_async_copy(
            proj_ref.at[pl.ds(*cut)], weights.at[pl.ds(*cut)], weights_sem.at[i]
        )
        for i, cut in enumerate(proj_cuts)
    ]
    for copy in row_copies + [gain_copy] + proj_copies[:3]:
        copy.start()

    tall = seq_len // hidden_parts
    for i, copy in enumerate(row_copies):
        copy.wait()
        for later in proj_copies[3 + 3 * i : 6 + 3 * i]:
            later.start()
        for start in range(i * tall, (i + 1) * tall, group):
            cut = pl.ds(start, group)
            squares = jnp.zeros((group, lane), jnp.float32)
            for k in range(0, width, lane):
                x = rows[cut, k : k + lane].astype(jnp.float32)
                squares = squares + x * x
            squares_ref[cut, :] = squares

    terms = jnp.concatenate(three_parts(squares_ref[...]), axis=1).astype(jnp.bfloat16)
    sums = lax.dot_general(
        jnp.ones((16, 3 * lane), jnp.bfloat16), terms, (((1,), (1,)), ((), ())),
        preferred_element_type=jnp.float32,
    )
    length = length_ref[0]
    one_share = 1.0 / jnp.full((1, 1), length, jnp.int32).astype(jnp.float32)
    position = lax.broadcasted_iota(jnp.int32, sums.shape, 1)
    share = jnp.where(position < length, one_share, 0.0)
    high, middle, low = three_parts(share * lax.rsqrt(sums / width + norm_eps))
    term = lax.broadcasted_iota(jnp.int32, sums.shape, 0)
    near = jnp.where(term == 0, high, jnp.where(term == 1, middle, jnp.where(term == 2, low, 0.0)))
    pooled = jnp.dot(near.astype(jnp.bfloat16), rows[...], preferred_element_type=jnp.float32)
    gain_copy.wait()
    scale = gain_at[...].astype(jnp.float32).reshape(1, width)
    scale_ref[...] = scale
    pooled = jnp.sum(pooled, axis=0, keepdims=True) * scale
    pooled = jnp.broadcast_to(pooled, (16, width)).astype(jnp.bfloat16)

    raw = jnp.zeros((16, emb_width), jnp.float32)
    for (at, deep), copy in zip(proj_cuts, proj_copies):
        copy.wait()
        raw = raw + jnp.dot(
            pooled[:, at : at + deep],
            weights[pl.ds(at, deep), :],
            preferred_element_type=jnp.float32,
        )
    raw_ref[...] = raw[:1]
    sheet = lax.broadcasted_iota(jnp.int32, (8, lane), 0)
    block = raw[:8, :lane]
    for k in range(1, emb_width // lane):
        block = jnp.where(sheet == k, raw[:8, k * lane : (k + 1) * lane], block)
    total = jnp.sum(jnp.sum(block * block, axis=1, keepdims=True), axis=0, keepdims=True)
    emb = (block * lax.rsqrt(total + norm_eps)).astype(jnp.bfloat16)
    copies_ref[...] = jnp.broadcast_to(emb[None], copies_ref.shape)


def grad_kernel(
    length_ref, held_ref, perm_ref, raw_ref, squares_ref, scale_ref, rows, weights,
    out_ref, loss_ref,
    wide, results, loss_at, results_sem, loss_sem,
):
    seq_len, width = rows.shape
    emb_width = weights.shape[1]
    seq_count = held_ref.shape[0]
    pair_count = perm_ref.shape[1]

    me = lax.axis_index(both)
    wide[...] = held_ref[...].astype(jnp.float32).reshape(wide.shape)
    sheets = emb_width // lane
    chunks = [wide[pl.ds(k, seq_count, stride=sheets), :] for k in range(sheets)]
    emb_f = jnp.concatenate(chunks, axis=1)
    emb = emb_f.astype(jnp.bfloat16)
    scores = inv_temp * lax.dot_general(
        emb, emb, (((1,), (1,)), ((), ())), preferred_element_type=jnp.float32
    )
    square = (seq_count, seq_count)
    row_id = lax.broadcasted_iota(jnp.int32, square, 0)
    col_id = lax.broadcasted_iota(jnp.int32, square, 1)
    across = (row_id < pair_count) != (col_id < pair_count)
    exp_scores = jnp.where(across, jnp.exp(jnp.where(across, scores, 0.0)), 0.0)
    totals = jnp.sum(exp_scores, axis=1, keepdims=True)
    own_col = jnp.sum(jnp.where(col_id == me, exp_scores, 0.0), axis=1, keepdims=True)
    own_total = jnp.sum(own_col, axis=0, keepdims=True)
    perm = perm_ref[...]
    pair_id = lax.broadcasted_iota(jnp.int32, perm.shape, 1)
    as_code = jnp.where(pair_id == me, perm + pair_count, 0)
    as_doc = jnp.where(perm == me - pair_count, pair_id, 0)
    partner = jnp.sum(
        jnp.where(me < pair_count, as_code, as_doc).astype(jnp.float32), axis=1, keepdims=True
    ).astype(jnp.int32)
    seq_id = lax.broadcasted_iota(jnp.int32, (seq_count, 1), 0)
    target = jnp.where(seq_id == partner, 2.0, 0.0)
    factors = own_col * (1.0 / own_total + 1.0 / totals) - target
    demb = (loss_scale * inv_temp) * jnp.sum(factors * emb_f, axis=0, keepdims=True)
    raw = raw_ref[...]
    magnitude = jnp.sqrt(jnp.sum(raw * raw, axis=1, keepdims=True) + norm_eps)
    unit = raw / magnitude
    projected = jnp.sum(unit * demb, axis=1, keepdims=True)
    grad_raw = (demb - unit * projected) / magnitude
    grad_raw = jnp.broadcast_to(grad_raw, (16, emb_width)).astype(jnp.bfloat16)

    own_row = grad_raw[:8].astype(jnp.float32)
    pieces = []
    for start in range(0, width, back_rows):
        middle = start + mxu_rows
        piece = lax.dot_general(
            grad_raw, weights[pl.ds(start, mxu_rows), :], (((1,), (1,)), ((), ())),
            preferred_element_type=jnp.float32,
        )
        pieces.append(piece[:8])
        for at in range(middle, min(start + back_rows, width), lane):
            part = jnp.zeros((lane // 8, 8, lane), jnp.float32)
            for k in range(0, emb_width, lane):
                block = weights[pl.ds(at, lane), k : k + lane].astype(jnp.float32)
                part = part + block.reshape(part.shape) * own_row[None, :, k : k + lane]
            piece = jnp.sum(part.reshape(lane, lane).T, axis=0, keepdims=True)
            pieces.append(jnp.broadcast_to(piece, (8, lane)))
    scaled = jnp.concatenate(pieces, axis=1) * scale_ref[...]

    matched = (row_id == perm_at_columns(perm, pair_count, seq_count)) & (col_id < pair_count)
    target_sum = jnp.sum(jnp.where(matched, scores, 0.0), axis=1, keepdims=True)
    terms = jnp.log(totals) - 2.0 * target_sum
    loss_at[...] = jnp.sum(terms, axis=0, keepdims=True) / seq_count
    loss_copy = pltpu.make_async_copy(loss_at, loss_ref, loss_sem)
    loss_copy.start()

    length = length_ref[0]
    one_share = 1.0 / jnp.full((1, 1), length, jnp.int32).astype(jnp.float32)
    mean = jnp.sum(squares_ref[...], axis=1, keepdims=True) / width
    inv_rms = lax.rsqrt(mean + norm_eps)
    position = lax.broadcasted_iota(jnp.int32, (seq_len, 1), 0)
    near_rows = jnp.where(position < length, one_share, 0.0) * inv_rms
    far_rows = near_rows * inv_rms * inv_rms / width

    nears, fars = [], []
    for start in range(0, seq_len, group):
        cut = pl.ds(start, group)
        dots = jnp.zeros((group // 8, 8, lane), jnp.float32)
        for k in range(0, width, lane):
            x = rows[cut, k : k + lane].astype(jnp.float32).reshape(dots.shape)
            dots = dots + x * scaled[None, :, k : k + lane]
        dot_rows = jnp.sum(dots.reshape(group, lane), axis=1, keepdims=True)
        far = far_rows[start : start + group] * dot_rows
        fars.append(jnp.broadcast_to(far, (group, lane)).reshape(dots.shape))
        near = near_rows[start : start + group]
        nears.append(jnp.broadcast_to(near, (group, lane)).reshape(dots.shape))

    out_copies = []
    for i, (at, tall) in enumerate(tall_parts(seq_len, out_rows)):
        rows_cut = pl.ds(at, tall)
        for start in range(at, at + tall, group):
            cut = pl.ds(start, group)
            near, far = nears[start // group], fars[start // group]
            for k in range(0, width, lane):
                x = rows[cut, k : k + lane].astype(jnp.float32).reshape(far.shape)
                result = near * scaled[None, :, k : k + lane] - far * x
                results[cut, k : k + lane] = result.reshape(group, lane).astype(jnp.bfloat16)
        out_copy = pltpu.make_async_copy(
            results.at[rows_cut], out_ref.at[0, rows_cut], results_sem.at[i]
        )
        out_copy.start()
        out_copies.append(out_copy)

    for out_copy in out_copies + [loss_copy]:
        out_copy.wait()


def perm_at_columns(perm, pair_count, seq_count):
    padding = jnp.full((1, seq_count - pair_count), -1, jnp.int32)
    return jnp.concatenate([perm + pair_count, padding], axis=1)


def body(hidden, lengths, pair_perm, norm_gain, projection):
    seq_len, width = hidden.shape[1:]
    emb_width = projection.shape[1]
    sheets = emb_width // lane
    seq_count = lax.axis_size(both)
    pair_count = seq_count // 2
    perm_row = pair_perm.reshape(1, pair_count)
    in_vmem = pl.BlockSpec(memory_space=pltpu.VMEM)
    anywhere = pl.BlockSpec(memory_space=pl.ANY)
    in_hbm = pl.BlockSpec(memory_space=pltpu.HBM)
    params = pltpu.CompilerParams(vmem_limit_bytes=16 * 1024 * 1024)
    copies, raw, squares, scale, rows, weights = pl.pallas_call(
        pool_kernel,
        out_shape=(
            pltpu.VMEM((seq_count, sheets, lane), jnp.bfloat16),
            pltpu.VMEM((1, emb_width), jnp.float32),
            pltpu.VMEM((seq_len, lane), jnp.float32),
            pltpu.VMEM((1, width), jnp.float32),
            pltpu.VMEM((seq_len, width), hidden.dtype),
            pltpu.VMEM((width, emb_width), projection.dtype),
        ),
        in_specs=[pl.BlockSpec(memory_space=pltpu.SMEM)] + [in_hbm] * 3,
        out_specs=(in_vmem,) * 6,
        scratch_shapes=[
            pltpu.VMEM((width,), norm_gain.dtype),
            pltpu.SemaphoreType.DMA((hidden_parts,)),
            pltpu.SemaphoreType.DMA((len(tall_parts(width, proj_rows)),)),
            pltpu.SemaphoreType.DMA,
        ],
        compiler_params=params,
        name="pool",
    )(lengths, *(
        pltpu.with_memory_space_constraint(x, pltpu.HBM)
        for x in (norm_gain, hidden, projection)
    ))

    held = lax.all_to_all(copies, both, 0, 0, tiled=True)

    grad, loss = pl.pallas_call(
        grad_kernel,
        out_shape=(
            jax.ShapeDtypeStruct(hidden.shape, jnp.bfloat16),
            jax.ShapeDtypeStruct((1, 1), jnp.float32),
        ),
        in_specs=[pl.BlockSpec(memory_space=pltpu.SMEM)] + [in_vmem] * 7,
        out_specs=(anywhere, anywhere),
        scratch_shapes=[
            pltpu.VMEM((seq_count * sheets, lane), jnp.float32),
            pltpu.VMEM((seq_len, width), jnp.bfloat16),
            pltpu.VMEM((1, 1), jnp.float32),
            pltpu.SemaphoreType.DMA((len(tall_parts(seq_len, out_rows)),)),
            pltpu.SemaphoreType.DMA,
        ],
        compiler_params=params,
        name="grad",
    )(lengths, *(
        pltpu.with_memory_space_constraint(x, pltpu.VMEM)
        for x in (held, perm_row, raw, squares, scale, rows, weights)
    ))
    return (grad, loss[0, 0])


def solution(mesh):
    in_specs = (P(both, None, None), P(both), P(), P(), P())
    out_specs = (P(both, None, None), P())
    return jax.shard_map(body, mesh=mesh, in_specs=in_specs, out_specs=out_specs, check_vma=False)
```

```python
import functools

import jax
import jax.numpy as jnp
from jax import lax
from jax.experimental import pallas as pl
from jax.experimental.pallas import tpu as pltpu
from jax.sharding import PartitionSpec as P

inv_temp = 20.0
loss_scale = 1024.0
norm_eps = 1e-06
both = ("section", "dp")

lane = 128
hidden_parts = 4
tall_rows = 1024
group = 32
back_parts = 4
mxu_rows = 256


def parts_of(total, count):
    step = total // count
    return [pl.ds(i * step, step) for i in range(count)]


def tall_parts(total):
    cuts = [(at, min(tall_rows, total - at)) for at in range(0, total, tall_rows)]
    at, tall = cuts.pop()
    return cuts + [(at, tall // 2), (at + tall // 2, tall - tall // 2)]


def out_cuts(total):
    quarter = total // 4
    return [(0, 2 * quarter), (2 * quarter, quarter), (3 * quarter, total - 3 * quarter)]


def three_parts(x):
    high = x.astype(jnp.bfloat16).astype(jnp.float32)
    middle = (x - high).astype(jnp.bfloat16).astype(jnp.float32)
    low = (x - high - middle).astype(jnp.bfloat16).astype(jnp.float32)
    return high, middle, low


def pool_kernel(
    length_ref, gain_ref, hidden_ref, proj_ref,
    copies_ref, raw_ref, squares_ref, scale_ref, rows, weights,
    gain_at, rows_sem, weights_sem, gain_sem,
):
    seq_len, width = rows.shape
    emb_width = weights.shape[1]
    gain_copy = pltpu.make_async_copy(gain_ref, gain_at, gain_sem)
    row_cuts = parts_of(seq_len, hidden_parts)
    proj_cuts = tall_parts(width)
    row_copies = [
        pltpu.make_async_copy(hidden_ref.at[0, cut], rows.at[cut], rows_sem.at[i])
        for i, cut in enumerate(row_cuts)
    ]
    proj_copies = [
        pltpu.make_async_copy(
            proj_ref.at[pl.ds(*cut)], weights.at[pl.ds(*cut)], weights_sem.at[i]
        )
        for i, cut in enumerate(proj_cuts)
    ]
    for copy in row_copies + [gain_copy] + proj_copies[:1]:
        copy.start()

    tall = seq_len // hidden_parts
    for i, copy in enumerate(row_copies):
        copy.wait()
        for later in proj_copies[1 + 2 * i : 3 + 2 * i]:
            later.start()
        for start in range(i * tall, (i + 1) * tall, group):
            cut = pl.ds(start, group)
            squares = jnp.zeros((group, lane), jnp.float32)
            for k in range(0, width, lane):
                x = rows[cut, k : k + lane].astype(jnp.float32)
                squares = squares + x * x
            squares_ref[cut, :] = squares

    terms = jnp.concatenate(three_parts(squares_ref[...]), axis=1).astype(jnp.bfloat16)
    sums = lax.dot_general(
        jnp.ones((16, 3 * lane), jnp.bfloat16), terms, (((1,), (1,)), ((), ())),
        preferred_element_type=jnp.float32,
    )
    length = length_ref[0]
    one_share = 1.0 / jnp.full((1, 1), length, jnp.int32).astype(jnp.float32)
    position = lax.broadcasted_iota(jnp.int32, sums.shape, 1)
    share = jnp.where(position < length, one_share, 0.0)
    high, middle, low = three_parts(share * lax.rsqrt(sums / width + norm_eps))
    term = lax.broadcasted_iota(jnp.int32, sums.shape, 0)
    near = jnp.where(term == 0, high, jnp.where(term == 1, middle, jnp.where(term == 2, low, 0.0)))
    pooled = jnp.dot(near.astype(jnp.bfloat16), rows[...], preferred_element_type=jnp.float32)
    gain_copy.wait()
    scale = gain_at[...].astype(jnp.float32).reshape(1, width)
    scale_ref[...] = scale
    pooled = jnp.sum(pooled, axis=0, keepdims=True) * scale
    pooled = jnp.broadcast_to(pooled, (16, width)).astype(jnp.bfloat16)

    raw = jnp.zeros((16, emb_width), jnp.float32)
    for (at, deep), copy in zip(proj_cuts, proj_copies):
        copy.wait()
        raw = raw + jnp.dot(
            pooled[:, at : at + deep],
            weights[pl.ds(at, deep), :],
            preferred_element_type=jnp.float32,
        )
    raw_ref[...] = raw[:1]
    sheet = lax.broadcasted_iota(jnp.int32, (8, lane), 0)
    block = raw[:8, :lane]
    for k in range(1, emb_width // lane):
        block = jnp.where(sheet == k, raw[:8, k * lane : (k + 1) * lane], block)
    total = jnp.sum(jnp.sum(block * block, axis=1, keepdims=True), axis=0, keepdims=True)
    emb = (block * lax.rsqrt(total + norm_eps)).astype(jnp.bfloat16)
    copies_ref[...] = jnp.broadcast_to(emb[None], copies_ref.shape)


def grad_kernel(
    length_ref, held_ref, perm_ref, raw_ref, squares_ref, scale_ref, rows, weights,
    out_ref, loss_ref,
    wide, results, loss_at, results_sem, loss_sem,
):
    seq_len, width = rows.shape
    emb_width = weights.shape[1]
    seq_count = held_ref.shape[0]
    pair_count = perm_ref.shape[1]

    me = lax.axis_index(both)
    wide[...] = held_ref[...].astype(jnp.float32).reshape(wide.shape)
    sheets = emb_width // lane
    chunks = [wide[pl.ds(k, seq_count, stride=sheets), :] for k in range(sheets)]
    emb_f = jnp.concatenate(chunks, axis=1)
    emb = emb_f.astype(jnp.bfloat16)
    scores = inv_temp * lax.dot_general(
        emb, emb, (((1,), (1,)), ((), ())), preferred_element_type=jnp.float32
    )
    square = (seq_count, seq_count)
    row_id = lax.broadcasted_iota(jnp.int32, square, 0)
    col_id = lax.broadcasted_iota(jnp.int32, square, 1)
    across = (row_id < pair_count) != (col_id < pair_count)
    exp_scores = jnp.where(across, jnp.exp(jnp.where(across, scores, 0.0)), 0.0)
    totals = jnp.sum(exp_scores, axis=1, keepdims=True)
    own_col = jnp.sum(jnp.where(col_id == me, exp_scores, 0.0), axis=1, keepdims=True)
    own_total = jnp.sum(own_col, axis=0, keepdims=True)
    perm = perm_ref[...]
    pair_id = lax.broadcasted_iota(jnp.int32, perm.shape, 1)
    as_code = jnp.where(pair_id == me, perm + pair_count, 0)
    as_doc = jnp.where(perm == me - pair_count, pair_id, 0)
    partner = jnp.sum(
        jnp.where(me < pair_count, as_code, as_doc).astype(jnp.float32), axis=1, keepdims=True
    ).astype(jnp.int32)
    seq_id = lax.broadcasted_iota(jnp.int32, (seq_count, 1), 0)
    target = jnp.where(seq_id == partner, 2.0, 0.0)
    factors = own_col * (1.0 / own_total + 1.0 / totals) - target
    demb = (loss_scale * inv_temp) * jnp.sum(factors * emb_f, axis=0, keepdims=True)
    raw = raw_ref[...]
    magnitude = jnp.sqrt(jnp.sum(raw * raw, axis=1, keepdims=True) + norm_eps)
    unit = raw / magnitude
    projected = jnp.sum(unit * demb, axis=1, keepdims=True)
    grad_raw = (demb - unit * projected) / magnitude
    grad_raw = jnp.broadcast_to(grad_raw, (16, emb_width)).astype(jnp.bfloat16)

    own_row = grad_raw[:8].astype(jnp.float32)
    pieces = []
    deep = width // back_parts
    for start in range(0, width, deep):
        middle = start + mxu_rows
        piece = lax.dot_general(
            grad_raw, weights[pl.ds(start, mxu_rows), :], (((1,), (1,)), ((), ())),
            preferred_element_type=jnp.float32,
        )
        pieces.append(piece[:8])
        for at in range(middle, start + deep, lane):
            part = jnp.zeros((lane // 8, 8, lane), jnp.float32)
            for k in range(0, emb_width, lane):
                block = weights[pl.ds(at, lane), k : k + lane].astype(jnp.float32)
                part = part + block.reshape(part.shape) * own_row[None, :, k : k + lane]
            piece = jnp.sum(part.reshape(lane, lane).T, axis=0, keepdims=True)
            pieces.append(jnp.broadcast_to(piece, (8, lane)))
    scaled = jnp.concatenate(pieces, axis=1) * scale_ref[...]

    matched = (row_id == perm_at_columns(perm, pair_count, seq_count)) & (col_id < pair_count)
    target_sum = jnp.sum(jnp.where(matched, scores, 0.0), axis=1, keepdims=True)
    terms = jnp.log(totals) - 2.0 * target_sum
    loss_at[...] = jnp.sum(terms, axis=0, keepdims=True) / seq_count
    loss_copy = pltpu.make_async_copy(loss_at, loss_ref, loss_sem)
    loss_copy.start()

    length = length_ref[0]
    one_share = 1.0 / jnp.full((1, 1), length, jnp.int32).astype(jnp.float32)
    mean = jnp.sum(squares_ref[...], axis=1, keepdims=True) / width
    inv_rms = lax.rsqrt(mean + norm_eps)
    position = lax.broadcasted_iota(jnp.int32, (seq_len, 1), 0)
    near_rows = jnp.where(position < length, one_share, 0.0) * inv_rms
    far_rows = near_rows * inv_rms * inv_rms / width

    nears, fars = [], []
    for start in range(0, seq_len, group):
        cut = pl.ds(start, group)
        dots = jnp.zeros((group // 8, 8, lane), jnp.float32)
        for k in range(0, width, lane):
            x = rows[cut, k : k + lane].astype(jnp.float32).reshape(dots.shape)
            dots = dots + x * scaled[None, :, k : k + lane]
        dot_rows = jnp.sum(dots.reshape(group, lane), axis=1, keepdims=True)
        far = far_rows[start : start + group] * dot_rows
        fars.append(jnp.broadcast_to(far, (group, lane)).reshape(dots.shape))
        near = near_rows[start : start + group]
        nears.append(jnp.broadcast_to(near, (group, lane)).reshape(dots.shape))

    out_copies = []
    for i, (at, tall) in enumerate(out_cuts(seq_len)):
        rows_cut = pl.ds(at, tall)
        for start in range(at, at + tall, group):
            cut = pl.ds(start, group)
            near, far = nears[start // group], fars[start // group]
            for k in range(0, width, lane):
                x = rows[cut, k : k + lane].astype(jnp.float32).reshape(far.shape)
                result = near * scaled[None, :, k : k + lane] - far * x
                results[cut, k : k + lane] = result.reshape(group, lane).astype(jnp.bfloat16)
        out_copy = pltpu.make_async_copy(
            results.at[rows_cut], out_ref.at[0, rows_cut], results_sem.at[i]
        )
        out_copy.start()
        out_copies.append(out_copy)

    for out_copy in out_copies + [loss_copy]:
        out_copy.wait()


def perm_at_columns(perm, pair_count, seq_count):
    padding = jnp.full((1, seq_count - pair_count), -1, jnp.int32)
    return jnp.concatenate([perm + pair_count, padding], axis=1)


def body(hidden, lengths, pair_perm, norm_gain, projection):
    seq_len, width = hidden.shape[1:]
    emb_width = projection.shape[1]
    sheets = emb_width // lane
    seq_count = lax.axis_size(both)
    pair_count = seq_count // 2
    perm_row = pair_perm.reshape(1, pair_count)
    in_vmem = pl.BlockSpec(memory_space=pltpu.VMEM)
    anywhere = pl.BlockSpec(memory_space=pl.ANY)
    in_hbm = pl.BlockSpec(memory_space=pltpu.HBM)
    params = pltpu.CompilerParams(vmem_limit_bytes=16 * 1024 * 1024)
    copies, raw, squares, scale, rows, weights = pl.pallas_call(
        pool_kernel,
        out_shape=(
            pltpu.VMEM((seq_count, sheets, lane), jnp.bfloat16),
            pltpu.VMEM((1, emb_width), jnp.float32),
            pltpu.VMEM((seq_len, lane), jnp.float32),
            pltpu.VMEM((1, width), jnp.float32),
            pltpu.VMEM((seq_len, width), hidden.dtype),
            pltpu.VMEM((width, emb_width), projection.dtype),
        ),
        in_specs=[pl.BlockSpec(memory_space=pltpu.SMEM)] + [in_hbm] * 3,
        out_specs=(in_vmem,) * 6,
        scratch_shapes=[
            pltpu.VMEM((width,), norm_gain.dtype),
            pltpu.SemaphoreType.DMA((hidden_parts,)),
            pltpu.SemaphoreType.DMA((len(tall_parts(width)),)),
            pltpu.SemaphoreType.DMA,
        ],
        compiler_params=params,
        name="pool",
    )(lengths, *(
        pltpu.with_memory_space_constraint(x, pltpu.HBM)
        for x in (norm_gain, hidden, projection)
    ))

    held = lax.all_to_all(copies, both, 0, 0, tiled=True)

    grad, loss = pl.pallas_call(
        grad_kernel,
        out_shape=(
            jax.ShapeDtypeStruct(hidden.shape, jnp.bfloat16),
            jax.ShapeDtypeStruct((1, 1), jnp.float32),
        ),
        in_specs=[pl.BlockSpec(memory_space=pltpu.SMEM)] + [in_vmem] * 7,
        out_specs=(anywhere, anywhere),
        scratch_shapes=[
            pltpu.VMEM((seq_count * sheets, lane), jnp.float32),
            pltpu.VMEM((seq_len, width), jnp.bfloat16),
            pltpu.VMEM((1, 1), jnp.float32),
            pltpu.SemaphoreType.DMA((len(out_cuts(seq_len)),)),
            pltpu.SemaphoreType.DMA,
        ],
        compiler_params=params,
        name="grad",
    )(lengths, *(
        pltpu.with_memory_space_constraint(x, pltpu.VMEM)
        for x in (held, perm_row, raw, squares, scale, rows, weights)
    ))
    return (grad, loss[0, 0])


def solution(mesh):
    in_specs = (P(both, None, None), P(both), P(), P(), P())
    out_specs = (P(both, None, None), P())
    return jax.shard_map(body, mesh=mesh, in_specs=in_specs, out_specs=out_specs, check_vma=False)
```

```python
import functools

import jax
import jax.numpy as jnp
from jax import lax
from jax.experimental import pallas as pl
from jax.experimental.pallas import tpu as pltpu
from jax.sharding import PartitionSpec as P

inv_temp = 20.0
loss_scale = 1024.0
norm_eps = 1e-06
both = ("section", "dp")

lane = 128
hidden_parts = 4
tall_rows = 512
group = 32
back_parts = 4
mxu_rows = 256


def parts_of(total, count):
    step = total // count
    return [pl.ds(i * step, step) for i in range(count)]


def tall_parts(total):
    cuts = [(at, min(tall_rows, total - at)) for at in range(0, total, tall_rows)]
    at, tall = cuts.pop()
    return cuts + [(at, tall // 2), (at + tall // 2, tall - tall // 2)]


def three_parts(x):
    high = x.astype(jnp.bfloat16).astype(jnp.float32)
    middle = (x - high).astype(jnp.bfloat16).astype(jnp.float32)
    low = (x - high - middle).astype(jnp.bfloat16).astype(jnp.float32)
    return high, middle, low


def pool_kernel(
    length_ref, gain_ref, hidden_ref, proj_ref,
    copies_ref, raw_ref, near_ref, far_ref, scale_ref, rows, weights,
    gain_at, squares_ref, rows_sem, weights_sem, gain_sem,
):
    seq_len, width = rows.shape
    emb_width = weights.shape[1]
    gain_copy = pltpu.make_async_copy(gain_ref, gain_at, gain_sem)
    row_cuts = parts_of(seq_len, hidden_parts)
    proj_cuts = tall_parts(width)
    row_copies = [
        pltpu.make_async_copy(hidden_ref.at[0, cut], rows.at[cut], rows_sem.at[i])
        for i, cut in enumerate(row_cuts)
    ]
    proj_copies = [
        pltpu.make_async_copy(
            proj_ref.at[pl.ds(*cut)], weights.at[pl.ds(*cut)], weights_sem.at[i]
        )
        for i, cut in enumerate(proj_cuts)
    ]
    for copy in row_copies + [gain_copy] + proj_copies[:2]:
        copy.start()

    tall = seq_len // hidden_parts
    for i, copy in enumerate(row_copies):
        copy.wait()
        for later in proj_copies[2 + 2 * i : 4 + 2 * i]:
            later.start()
        for start in range(i * tall, (i + 1) * tall, group):
            cut = pl.ds(start, group)
            squares = jnp.zeros((group, lane), jnp.float32)
            for k in range(0, width, lane):
                x = rows[cut, k : k + lane].astype(jnp.float32)
                squares = squares + x * x
            squares_ref[cut, :] = squares

    terms = jnp.concatenate(three_parts(squares_ref[...]), axis=1).astype(jnp.bfloat16)
    sums = lax.dot_general(
        jnp.ones((16, 3 * lane), jnp.bfloat16), terms, (((1,), (1,)), ((), ())),
        preferred_element_type=jnp.float32,
    )
    length = length_ref[0]
    one_share = 1.0 / jnp.full((1, 1), length, jnp.int32).astype(jnp.float32)
    position = lax.broadcasted_iota(jnp.int32, sums.shape, 1)
    share = jnp.where(position < length, one_share, 0.0)
    high, middle, low = three_parts(share * lax.rsqrt(sums / width + norm_eps))
    term = lax.broadcasted_iota(jnp.int32, sums.shape, 0)
    near = jnp.where(term == 0, high, jnp.where(term == 1, middle, jnp.where(term == 2, low, 0.0)))
    pooled = jnp.dot(near.astype(jnp.bfloat16), rows[...], preferred_element_type=jnp.float32)
    gain_copy.wait()
    scale = gain_at[...].astype(jnp.float32).reshape(1, width)
    scale_ref[...] = scale
    pooled = jnp.sum(pooled, axis=0, keepdims=True) * scale
    pooled = jnp.broadcast_to(pooled, (16, width)).astype(jnp.bfloat16)

    raw = jnp.zeros((16, emb_width), jnp.float32)
    for (at, deep), copy in zip(proj_cuts, proj_copies):
        copy.wait()
        raw = raw + jnp.dot(
            pooled[:, at : at + deep],
            weights[pl.ds(at, deep), :],
            preferred_element_type=jnp.float32,
        )
        if at == 0:
            mean = jnp.sum(squares_ref[...], axis=1, keepdims=True) / width
            inv_rms = jnp.broadcast_to(lax.rsqrt(mean + norm_eps), (seq_len, lane))
            position = lax.broadcasted_iota(jnp.int32, (seq_len, lane), 0)
            near_rows = jnp.where(position < length, one_share, 0.0) * inv_rms
            near_ref[...] = near_rows
            far_ref[...] = near_rows * inv_rms * inv_rms / width
    raw_ref[...] = raw[:1]
    sheet = lax.broadcasted_iota(jnp.int32, (8, lane), 0)
    block = raw[:8, :lane]
    for k in range(1, emb_width // lane):
        block = jnp.where(sheet == k, raw[:8, k * lane : (k + 1) * lane], block)
    total = jnp.sum(jnp.sum(block * block, axis=1, keepdims=True), axis=0, keepdims=True)
    emb = (block * lax.rsqrt(total + norm_eps)).astype(jnp.bfloat16)
    copies_ref[...] = jnp.broadcast_to(emb[None], copies_ref.shape)


def grad_kernel(
    held_ref, perm_ref, raw_ref, near_ref, far_ref, scale_ref, rows, weights,
    out_ref, loss_ref,
    wide, results, loss_at, results_sem, loss_sem,
):
    seq_len, width = rows.shape
    emb_width = weights.shape[1]
    seq_count = held_ref.shape[0]
    pair_count = perm_ref.shape[1]
    row_cuts = parts_of(seq_len, hidden_parts)

    me = lax.axis_index(both)
    wide[...] = held_ref[...].astype(jnp.float32).reshape(wide.shape)
    sheets = emb_width // lane
    chunks = [wide[pl.ds(k, seq_count, stride=sheets), :] for k in range(sheets)]
    emb_f = jnp.concatenate(chunks, axis=1)
    emb = emb_f.astype(jnp.bfloat16)
    scores = inv_temp * lax.dot_general(
        emb, emb, (((1,), (1,)), ((), ())), preferred_element_type=jnp.float32
    )
    square = (seq_count, seq_count)
    row_id = lax.broadcasted_iota(jnp.int32, square, 0)
    col_id = lax.broadcasted_iota(jnp.int32, square, 1)
    across = (row_id < pair_count) != (col_id < pair_count)
    exp_scores = jnp.where(across, jnp.exp(jnp.where(across, scores, 0.0)), 0.0)
    totals = jnp.sum(exp_scores, axis=1, keepdims=True)
    own_col = jnp.sum(jnp.where(col_id == me, exp_scores, 0.0), axis=1, keepdims=True)
    own_total = jnp.sum(own_col, axis=0, keepdims=True)
    perm = perm_ref[...]
    pair_id = lax.broadcasted_iota(jnp.int32, perm.shape, 1)
    as_code = jnp.where(pair_id == me, perm + pair_count, 0)
    as_doc = jnp.where(perm == me - pair_count, pair_id, 0)
    partner = jnp.sum(
        jnp.where(me < pair_count, as_code, as_doc).astype(jnp.float32), axis=1, keepdims=True
    ).astype(jnp.int32)
    seq_id = lax.broadcasted_iota(jnp.int32, (seq_count, 1), 0)
    target = jnp.where(seq_id == partner, 2.0, 0.0)
    factors = own_col * (1.0 / own_total + 1.0 / totals) - target
    demb = (loss_scale * inv_temp) * jnp.sum(factors * emb_f, axis=0, keepdims=True)
    raw = raw_ref[...]
    magnitude = jnp.sqrt(jnp.sum(raw * raw, axis=1, keepdims=True) + norm_eps)
    unit = raw / magnitude
    projected = jnp.sum(unit * demb, axis=1, keepdims=True)
    grad_raw = (demb - unit * projected) / magnitude
    grad_raw = jnp.broadcast_to(grad_raw, (16, emb_width)).astype(jnp.bfloat16)

    own_row = grad_raw[:8].astype(jnp.float32)
    pieces = []
    deep = width // back_parts
    for start in range(0, width, deep):
        middle = start + mxu_rows
        piece = lax.dot_general(
            grad_raw, weights[pl.ds(start, mxu_rows), :], (((1,), (1,)), ((), ())),
            preferred_element_type=jnp.float32,
        )
        pieces.append(piece[:8])
        for at in range(middle, start + deep, lane):
            part = jnp.zeros((lane // 8, 8, lane), jnp.float32)
            for k in range(0, emb_width, lane):
                block = weights[pl.ds(at, lane), k : k + lane].astype(jnp.float32)
                part = part + block.reshape(part.shape) * own_row[None, :, k : k + lane]
            piece = jnp.sum(part.reshape(lane, lane).T, axis=0, keepdims=True)
            pieces.append(jnp.broadcast_to(piece, (8, lane)))
    scaled = jnp.concatenate(pieces, axis=1) * scale_ref[...]

    matched = (row_id == perm_at_columns(perm, pair_count, seq_count)) & (col_id < pair_count)
    target_sum = jnp.sum(jnp.where(matched, scores, 0.0), axis=1, keepdims=True)
    terms = jnp.log(totals) - 2.0 * target_sum
    loss_at[...] = jnp.sum(terms, axis=0, keepdims=True) / seq_count
    loss_copy = pltpu.make_async_copy(loss_at, loss_ref, loss_sem)
    loss_copy.start()

    nears, fars = [], []
    for start in range(0, seq_len, group):
        cut = pl.ds(start, group)
        dots = jnp.zeros((group // 8, 8, lane), jnp.float32)
        for k in range(0, width, lane):
            x = rows[cut, k : k + lane].astype(jnp.float32).reshape(dots.shape)
            dots = dots + x * scaled[None, :, k : k + lane]
        dot_rows = jnp.sum(dots.reshape(group, lane), axis=1, keepdims=True)
        far = far_ref[cut, :] * jnp.broadcast_to(dot_rows, (group, lane))
        fars.append(far.reshape(dots.shape))
        nears.append(near_ref[cut, :].reshape(dots.shape))

    tall = seq_len // hidden_parts
    out_copies = []
    for i, rows_cut in enumerate(row_cuts):
        for start in range(i * tall, (i + 1) * tall, group):
            cut = pl.ds(start, group)
            near, far = nears[start // group], fars[start // group]
            for k in range(0, width, lane):
                x = rows[cut, k : k + lane].astype(jnp.float32).reshape(far.shape)
                result = near * scaled[None, :, k : k + lane] - far * x
                results[cut, k : k + lane] = result.reshape(group, lane).astype(jnp.bfloat16)
        out_copy = pltpu.make_async_copy(
            results.at[rows_cut], out_ref.at[0, rows_cut], results_sem.at[i]
        )
        out_copy.start()
        out_copies.append(out_copy)

    for out_copy in out_copies + [loss_copy]:
        out_copy.wait()


def perm_at_columns(perm, pair_count, seq_count):
    padding = jnp.full((1, seq_count - pair_count), -1, jnp.int32)
    return jnp.concatenate([perm + pair_count, padding], axis=1)


def body(hidden, lengths, pair_perm, norm_gain, projection):
    seq_len, width = hidden.shape[1:]
    emb_width = projection.shape[1]
    sheets = emb_width // lane
    seq_count = lax.axis_size(both)
    pair_count = seq_count // 2
    perm_row = pair_perm.reshape(1, pair_count)
    in_vmem = pl.BlockSpec(memory_space=pltpu.VMEM)
    anywhere = pl.BlockSpec(memory_space=pl.ANY)
    in_hbm = pl.BlockSpec(memory_space=pltpu.HBM)
    params = pltpu.CompilerParams(vmem_limit_bytes=16 * 1024 * 1024)
    copies, raw, near, far, scale, rows, weights = pl.pallas_call(
        pool_kernel,
        out_shape=(
            pltpu.VMEM((seq_count, sheets, lane), jnp.bfloat16),
            pltpu.VMEM((1, emb_width), jnp.float32),
            pltpu.VMEM((seq_len, lane), jnp.float32),
            pltpu.VMEM((seq_len, lane), jnp.float32),
            pltpu.VMEM((1, width), jnp.float32),
            pltpu.VMEM((seq_len, width), hidden.dtype),
            pltpu.VMEM((width, emb_width), projection.dtype),
        ),
        in_specs=[pl.BlockSpec(memory_space=pltpu.SMEM)] + [in_hbm] * 3,
        out_specs=(in_vmem,) * 7,
        scratch_shapes=[
            pltpu.VMEM((width,), norm_gain.dtype),
            pltpu.VMEM((seq_len, lane), jnp.float32),
            pltpu.SemaphoreType.DMA((hidden_parts,)),
            pltpu.SemaphoreType.DMA((len(tall_parts(width)),)),
            pltpu.SemaphoreType.DMA,
        ],
        compiler_params=params,
        name="pool",
    )(lengths, *(
        pltpu.with_memory_space_constraint(x, pltpu.HBM)
        for x in (norm_gain, hidden, projection)
    ))

    held = lax.all_to_all(copies, both, 0, 0, tiled=True)

    grad, loss = pl.pallas_call(
        grad_kernel,
        out_shape=(
            jax.ShapeDtypeStruct(hidden.shape, jnp.bfloat16),
            jax.ShapeDtypeStruct((1, 1), jnp.float32),
        ),
        in_specs=[in_vmem] * 8,
        out_specs=(anywhere, anywhere),
        scratch_shapes=[
            pltpu.VMEM((seq_count * sheets, lane), jnp.float32),
            pltpu.VMEM((seq_len, width), jnp.bfloat16),
            pltpu.VMEM((1, 1), jnp.float32),
            pltpu.SemaphoreType.DMA((hidden_parts,)),
            pltpu.SemaphoreType.DMA,
        ],
        compiler_params=params,
        name="grad",
    )(*(
        pltpu.with_memory_space_constraint(x, pltpu.VMEM)
        for x in (held, perm_row, raw, near, far, scale, rows, weights)
    ))
    return (grad, loss[0, 0])


def solution(mesh):
    in_specs = (P(both, None, None), P(both), P(), P(), P())
    out_specs = (P(both, None, None), P())
    return jax.shard_map(body, mesh=mesh, in_specs=in_specs, out_specs=out_specs, check_vma=False)
```

```python
import functools

import jax
import jax.numpy as jnp
from jax import lax
from jax.experimental import pallas as pl
from jax.experimental.pallas import tpu as pltpu
from jax.sharding import PartitionSpec as P

inv_temp = 20.0
loss_scale = 1024.0
norm_eps = 1e-06
both = ("section", "dp")

lane = 128
hidden_parts = 4
tall_rows = 512
group = 32
back_parts = 4
mxu_rows = 256


def parts_of(total, count):
    step = total // count
    return [pl.ds(i * step, step) for i in range(count)]


def tall_parts(total):
    cuts = [(at, min(tall_rows, total - at)) for at in range(0, total, tall_rows)]
    at, tall = cuts.pop()
    return cuts + [(at, tall // 2), (at + tall // 2, tall - tall // 2)]


def out_cuts(total):
    tall = 2 * group
    return [(0, group), (group, group)] + [(at, tall) for at in range(tall, total, tall)]


def three_parts(x):
    high = x.astype(jnp.bfloat16).astype(jnp.float32)
    middle = (x - high).astype(jnp.bfloat16).astype(jnp.float32)
    low = (x - high - middle).astype(jnp.bfloat16).astype(jnp.float32)
    return high, middle, low


def pool_kernel(
    length_ref, gain_ref, hidden_ref, proj_ref,
    copies_ref, raw_ref, squares_ref, scale_ref, rows, weights,
    gain_at, rows_sem, weights_sem, gain_sem,
):
    seq_len, width = rows.shape
    emb_width = weights.shape[1]
    gain_copy = pltpu.make_async_copy(gain_ref, gain_at, gain_sem)
    row_cuts = parts_of(seq_len, hidden_parts)
    proj_cuts = tall_parts(width)
    row_copies = [
        pltpu.make_async_copy(hidden_ref.at[0, cut], rows.at[cut], rows_sem.at[i])
        for i, cut in enumerate(row_cuts)
    ]
    proj_copies = [
        pltpu.make_async_copy(
            proj_ref.at[pl.ds(*cut)], weights.at[pl.ds(*cut)], weights_sem.at[i]
        )
        for i, cut in enumerate(proj_cuts)
    ]
    for copy in row_copies + [gain_copy] + proj_copies[:2]:
        copy.start()

    tall = seq_len // hidden_parts
    for i, copy in enumerate(row_copies):
        copy.wait()
        for later in proj_copies[2 + 2 * i : 4 + 2 * i]:
            later.start()
        for start in range(i * tall, (i + 1) * tall, group):
            cut = pl.ds(start, group)
            squares = jnp.zeros((group, lane), jnp.float32)
            for k in range(0, width, lane):
                x = rows[cut, k : k + lane].astype(jnp.float32)
                squares = squares + x * x
            squares_ref[cut, :] = squares

    terms = jnp.concatenate(three_parts(squares_ref[...]), axis=1).astype(jnp.bfloat16)
    sums = lax.dot_general(
        jnp.ones((16, 3 * lane), jnp.bfloat16), terms, (((1,), (1,)), ((), ())),
        preferred_element_type=jnp.float32,
    )
    length = length_ref[0]
    one_share = 1.0 / jnp.full((1, 1), length, jnp.int32).astype(jnp.float32)
    position = lax.broadcasted_iota(jnp.int32, sums.shape, 1)
    share = jnp.where(position < length, one_share, 0.0)
    high, middle, low = three_parts(share * lax.rsqrt(sums / width + norm_eps))
    term = lax.broadcasted_iota(jnp.int32, sums.shape, 0)
    near = jnp.where(term == 0, high, jnp.where(term == 1, middle, jnp.where(term == 2, low, 0.0)))
    pooled = jnp.dot(near.astype(jnp.bfloat16), rows[...], preferred_element_type=jnp.float32)
    gain_copy.wait()
    scale = gain_at[...].astype(jnp.float32).reshape(1, width)
    scale_ref[...] = scale
    pooled = jnp.sum(pooled, axis=0, keepdims=True) * scale
    pooled = jnp.broadcast_to(pooled, (8, width)).astype(jnp.bfloat16)

    raw = jnp.zeros((8, emb_width), jnp.float32)
    for (at, deep), copy in zip(proj_cuts, proj_copies):
        copy.wait()
        raw = raw + jnp.dot(
            pooled[:, at : at + deep],
            weights[pl.ds(at, deep), :],
            preferred_element_type=jnp.float32,
        )
    raw_ref[...] = raw[:1]
    sheet = lax.broadcasted_iota(jnp.int32, (8, lane), 0)
    block = raw[:8, :lane]
    for k in range(1, emb_width // lane):
        block = jnp.where(sheet == k, raw[:8, k * lane : (k + 1) * lane], block)
    total = jnp.sum(jnp.sum(block * block, axis=1, keepdims=True), axis=0, keepdims=True)
    emb = (block * lax.rsqrt(total + norm_eps)).astype(jnp.bfloat16)
    copies_ref[...] = jnp.broadcast_to(emb[None], copies_ref.shape)


def grad_kernel(
    length_ref, held_ref, perm_ref, raw_ref, squares_ref, scale_ref, rows, weights,
    out_ref, loss_ref,
    wide, results, loss_at, results_sem, loss_sem,
):
    seq_len, width = rows.shape
    emb_width = weights.shape[1]
    seq_count = held_ref.shape[0]
    pair_count = perm_ref.shape[1]

    me = lax.axis_index(both)
    wide[...] = held_ref[...].astype(jnp.float32).reshape(wide.shape)
    sheets = emb_width // lane
    chunks = [wide[pl.ds(k, seq_count, stride=sheets), :] for k in range(sheets)]
    emb_f = jnp.concatenate(chunks, axis=1)
    emb = emb_f.astype(jnp.bfloat16)
    scores = inv_temp * lax.dot_general(
        emb, emb, (((1,), (1,)), ((), ())), preferred_element_type=jnp.float32
    )
    square = (seq_count, seq_count)
    row_id = lax.broadcasted_iota(jnp.int32, square, 0)
    col_id = lax.broadcasted_iota(jnp.int32, square, 1)
    across = (row_id < pair_count) != (col_id < pair_count)
    exp_scores = jnp.where(across, jnp.exp(jnp.where(across, scores, 0.0)), 0.0)
    totals = jnp.sum(exp_scores, axis=1, keepdims=True)
    own_col = jnp.sum(jnp.where(col_id == me, exp_scores, 0.0), axis=1, keepdims=True)
    own_total = jnp.sum(own_col, axis=0, keepdims=True)
    perm = perm_ref[...]
    pair_id = lax.broadcasted_iota(jnp.int32, perm.shape, 1)
    as_code = jnp.where(pair_id == me, perm + pair_count, 0)
    as_doc = jnp.where(perm == me - pair_count, pair_id, 0)
    partner = jnp.sum(
        jnp.where(me < pair_count, as_code, as_doc).astype(jnp.float32), axis=1, keepdims=True
    ).astype(jnp.int32)
    seq_id = lax.broadcasted_iota(jnp.int32, (seq_count, 1), 0)
    target = jnp.where(seq_id == partner, 2.0, 0.0)
    factors = own_col * (1.0 / own_total + 1.0 / totals) - target
    demb = (loss_scale * inv_temp) * jnp.sum(factors * emb_f, axis=0, keepdims=True)
    raw = raw_ref[...]
    magnitude = jnp.sqrt(jnp.sum(raw * raw, axis=1, keepdims=True) + norm_eps)
    unit = raw / magnitude
    projected = jnp.sum(unit * demb, axis=1, keepdims=True)
    grad_raw = (demb - unit * projected) / magnitude
    grad_raw = jnp.broadcast_to(grad_raw, (8, emb_width)).astype(jnp.bfloat16)

    own_row = grad_raw[:8].astype(jnp.float32)
    pieces = []
    deep = width // back_parts
    for start in range(0, width, deep):
        middle = start + mxu_rows
        piece = lax.dot_general(
            grad_raw, weights[pl.ds(start, mxu_rows), :], (((1,), (1,)), ((), ())),
            preferred_element_type=jnp.float32,
        )
        pieces.append(piece[:8])
        for at in range(middle, start + deep, lane):
            part = jnp.zeros((lane // 8, 8, lane), jnp.float32)
            for k in range(0, emb_width, lane):
                block = weights[pl.ds(at, lane), k : k + lane].astype(jnp.float32)
                part = part + block.reshape(part.shape) * own_row[None, :, k : k + lane]
            piece = jnp.sum(part.reshape(lane, lane).T, axis=0, keepdims=True)
            pieces.append(jnp.broadcast_to(piece, (8, lane)))
    scaled = jnp.concatenate(pieces, axis=1) * scale_ref[...]

    matched = (row_id == perm_at_columns(perm, pair_count, seq_count)) & (col_id < pair_count)
    target_sum = jnp.sum(jnp.where(matched, scores, 0.0), axis=1, keepdims=True)
    terms = jnp.log(totals) - 2.0 * target_sum
    loss_at[...] = jnp.sum(terms, axis=0, keepdims=True) / seq_count
    loss_copy = pltpu.make_async_copy(loss_at, loss_ref, loss_sem)
    loss_copy.start()

    length = length_ref[0]
    one_share = 1.0 / jnp.full((1, 1), length, jnp.int32).astype(jnp.float32)
    mean = jnp.sum(squares_ref[...], axis=1, keepdims=True) / width
    inv_rms = lax.rsqrt(mean + norm_eps)
    position = lax.broadcasted_iota(jnp.int32, (seq_len, 1), 0)
    near_rows = jnp.where(position < length, one_share, 0.0) * inv_rms
    far_rows = near_rows * inv_rms * inv_rms / width

    nears, fars = [], []
    for start in range(0, seq_len, group):
        cut = pl.ds(start, group)
        dots = jnp.zeros((group // 8, 8, lane), jnp.float32)
        for k in range(0, width, lane):
            x = rows[cut, k : k + lane].astype(jnp.float32).reshape(dots.shape)
            dots = dots + x * scaled[None, :, k : k + lane]
        dot_rows = jnp.sum(dots.reshape(group, lane), axis=1, keepdims=True)
        far = far_rows[start : start + group] * dot_rows
        fars.append(jnp.broadcast_to(far, (group, lane)).reshape(dots.shape))
        near = near_rows[start : start + group]
        nears.append(jnp.broadcast_to(near, (group, lane)).reshape(dots.shape))

    out_copies = []
    for i, (at, tall) in enumerate(out_cuts(seq_len)):
        rows_cut = pl.ds(at, tall)
        for start in range(at, at + tall, group):
            cut = pl.ds(start, group)
            near, far = nears[start // group], fars[start // group]
            for k in range(0, width, lane):
                x = rows[cut, k : k + lane].astype(jnp.float32).reshape(far.shape)
                result = near * scaled[None, :, k : k + lane] - far * x
                results[cut, k : k + lane] = result.reshape(group, lane).astype(jnp.bfloat16)
        out_copy = pltpu.make_async_copy(
            results.at[rows_cut], out_ref.at[0, rows_cut], results_sem.at[i]
        )
        out_copy.start()
        out_copies.append(out_copy)

    for out_copy in out_copies + [loss_copy]:
        out_copy.wait()


def perm_at_columns(perm, pair_count, seq_count):
    padding = jnp.full((1, seq_count - pair_count), -1, jnp.int32)
    return jnp.concatenate([perm + pair_count, padding], axis=1)


def body(hidden, lengths, pair_perm, norm_gain, projection):
    seq_len, width = hidden.shape[1:]
    emb_width = projection.shape[1]
    sheets = emb_width // lane
    seq_count = lax.axis_size(both)
    pair_count = seq_count // 2
    perm_row = pair_perm.reshape(1, pair_count)
    in_vmem = pl.BlockSpec(memory_space=pltpu.VMEM)
    anywhere = pl.BlockSpec(memory_space=pl.ANY)
    in_hbm = pl.BlockSpec(memory_space=pltpu.HBM)
    params = pltpu.CompilerParams(vmem_limit_bytes=16 * 1024 * 1024)
    copies, raw, squares, scale, rows, weights = pl.pallas_call(
        pool_kernel,
        out_shape=(
            pltpu.VMEM((seq_count, sheets, lane), jnp.bfloat16),
            pltpu.VMEM((1, emb_width), jnp.float32),
            pltpu.VMEM((seq_len, lane), jnp.float32),
            pltpu.VMEM((1, width), jnp.float32),
            pltpu.VMEM((seq_len, width), hidden.dtype),
            pltpu.VMEM((width, emb_width), projection.dtype),
        ),
        in_specs=[pl.BlockSpec(memory_space=pltpu.SMEM)] + [in_hbm] * 3,
        out_specs=(in_vmem,) * 6,
        scratch_shapes=[
            pltpu.VMEM((width,), norm_gain.dtype),
            pltpu.SemaphoreType.DMA((hidden_parts,)),
            pltpu.SemaphoreType.DMA((len(tall_parts(width)),)),
            pltpu.SemaphoreType.DMA,
        ],
        compiler_params=params,
        name="pool",
    )(lengths, *(
        pltpu.with_memory_space_constraint(x, pltpu.HBM)
        for x in (norm_gain, hidden, projection)
    ))

    held = lax.all_to_all(copies, both, 0, 0, tiled=True)

    grad, loss = pl.pallas_call(
        grad_kernel,
        out_shape=(
            jax.ShapeDtypeStruct(hidden.shape, jnp.bfloat16),
            jax.ShapeDtypeStruct((1, 1), jnp.float32),
        ),
        in_specs=[pl.BlockSpec(memory_space=pltpu.SMEM)] + [in_vmem] * 7,
        out_specs=(anywhere, anywhere),
        scratch_shapes=[
            pltpu.VMEM((seq_count * sheets, lane), jnp.float32),
            pltpu.VMEM((seq_len, width), jnp.bfloat16),
            pltpu.VMEM((1, 1), jnp.float32),
            pltpu.SemaphoreType.DMA((len(out_cuts(seq_len)),)),
            pltpu.SemaphoreType.DMA,
        ],
        compiler_params=params,
        name="grad",
    )(lengths, *(
        pltpu.with_memory_space_constraint(x, pltpu.VMEM)
        for x in (held, perm_row, raw, squares, scale, rows, weights)
    ))
    return (grad, loss[0, 0])


def solution(mesh):
    in_specs = (P(both, None, None), P(both), P(), P(), P())
    out_specs = (P(both, None, None), P())
    return jax.shard_map(body, mesh=mesh, in_specs=in_specs, out_specs=out_specs, check_vma=False)
```
